128 devices in a mesh: gy: 8 (over z, y_lo), gx: 16 (over x, y_hi, core).
Axes of the slice: x: 4, y: 4 (y_hi: 2, y_lo: 2; y = y_hi * 2 + y_lo), z: 4, core: 2. Of those that a mesh axis runs over, the one named last changes fastest.
Arguments:
- radar_input: bfloat16 [512, 1024, 256], P('gy', 'gx'), may hold values from -6 to 6
- conv_weight: bfloat16 [3, 3, 256, 256], replicated, may hold values from -0.125 to 0.125
- conv_bias: float32 [256], replicated, may hold values from -3 to 3
- row_gain: float32 [256], replicated, may hold values from 0.1 to 1.9
- row_qkv: bfloat16 [256, 768], replicated, may hold values from -8 to 8
- row_out: bfloat16 [256, 256], replicated, may hold values from -0.375 to 0.375
- col_gain: float32 [256], replicated, may hold values from 0.1 to 1.9
- col_qkv: bfloat16 [256, 768], replicated, may hold values from -8 to 8
- col_out: bfloat16 [256, 256], replicated, may hold values from -0.375 to 0.375
Outputs:
- block_output: bfloat16 [512, 1024, 256], P('gy', 'gx')
The draws below stay inside these ranges and needn't reach their ends.
All inputs are finite; a program needn't handle non-finite values.
Results may differ from the reference program's by a relative error of at most 0.012.
Values may be sent and summed in bfloat16 or wider, within the bound.
No kernel may reach another device: no remote copies, remote signals or barrier semaphores. Data moves between devices by JAX's collectives and lax.ppermute only.
A program may use at most 128 MiB of HBM per device.

```python
import jax
import jax.numpy as jnp
from jax import lax

C = 256
HEADS = 8
H = 512
W = 1024


def base_matrix(key):
    return jnp.clip(jax.random.normal(key, (C, 3 * C), jnp.float32), -6.0, 6.0) * C ** (-0.5)


def draw_row_qkv(key, part):
    key = jax.random.fold_in(key, 11)
    matrix = base_matrix(key)
    return matrix.astype(jnp.bfloat16)


def draw_col_qkv(key, part):
    key = jax.random.fold_in(key, 23)
    matrix = base_matrix(key)
    return matrix.astype(jnp.bfloat16)


def shard_levels(own_key, dims, shards, low, high):
    def one(axis_at, blocks):
        draws = jax.random.uniform(jax.random.fold_in(jax.random.fold_in(own_key, 6), axis_at), (blocks,), jnp.float32, low / len(shards), high / len(shards))
        return jnp.repeat(jnp.exp(draws), dims[axis_at] // blocks).reshape((-1,) + (1,) * (len(dims) - axis_at - 1))

    loudness = one(*shards[0])
    for cut in shards[1:]:
        loudness = loudness * one(*cut)
    return loudness


def bell_draw(key, extent, scale, most, cuts=(), kind=jnp.bfloat16):
    factor_of = shard_levels(key, extent, cuts, -0.22, 0.18) if cuts else 1.0
    entries = jax.random.normal(key, extent, jnp.float32) * scale * factor_of
    return jnp.minimum(jnp.maximum(entries, -most), most).astype(kind)


def setup_inputs(seed: int = 0) -> dict:
    key_list = jax.random.split(jax.random.key(seed), 10)
    return {
        "radar_input": bell_draw(key_list[0], (H, W, C), 1.0, 6.0, ((0, 8), (1, 16))),
        "conv_weight": bell_draw(key_list[1], (3, 3, C, C), (9 * C) ** -0.5, 0.125),
        "conv_bias": bell_draw(key_list[2], (C,), 0.5, 3.0, (), jnp.float32),
        "row_gain": jnp.clip(1.0 + 0.18 * jax.random.normal(key_list[3], (C,), jnp.float32), 0.1, 1.9),
        "row_qkv": draw_row_qkv(jax.random.fold_in(key_list[9], 71), 0),
        "row_out": bell_draw(key_list[5], (C, C), C ** -0.5, 0.375),
        "col_gain": jnp.clip(1.0 + 0.18 * jax.random.normal(key_list[6], (C,), jnp.float32), 0.1, 1.9),
        "col_qkv": draw_col_qkv(jax.random.fold_in(key_list[9], 71), 0),
        "col_out": bell_draw(key_list[8], (C, C), C ** -0.5, 0.375),
    }


def layer_norm(grid, gain):
    values = grid.astype(jnp.float32)
    center = lax.optimization_barrier(jnp.mean(values, axis=-1, keepdims=True))
    spread = lax.optimization_barrier(jnp.mean((values - center) ** 2, axis=-1, keepdims=True))
    return ((values - center) * lax.rsqrt(spread + 1e-05) * gain).astype(jnp.bfloat16)

def convolve(padded, source, conv_weight, conv_bias):
    rows, cols, chans = source.shape
    total = jnp.zeros((rows * cols, conv_weight.shape[3]), jnp.float32)
    for dy in range(3):
        for dx in range(3):
            window = padded[dy:dy + rows, dx:dx + cols].reshape(rows * cols, chans)
            total = total + jnp.dot(window, conv_weight[dy, dx], preferred_element_type=jnp.float32)
    pre = total.reshape(rows, cols, -1) + conv_bias
    return (source.astype(jnp.float32) + jax.nn.gelu(pre)).astype(jnp.bfloat16)

def sequence_attention(queries, keys, values):
    length, chans = queries.shape
    heads = HEADS
    width = chans // heads
    qh = queries.reshape(length, heads, width).astype(jnp.float32)
    kh = keys.reshape(length, heads, width).astype(jnp.float32)
    vh = values.reshape(length, heads, width).astype(jnp.float32)
    block = min(length, 512)
    pieces = []
    for start in range(0, length, block):
        scores = jnp.einsum('qhd,khd->hqk', qh[start:start + block], kh) * width ** (-0.5)
        top = lax.optimization_barrier(jnp.max(scores, axis=-1, keepdims=True))
        expo = jnp.exp(scores - top)
        weights = (expo / lax.optimization_barrier(jnp.sum(expo, axis=-1, keepdims=True))).astype(jnp.bfloat16)
        mixed = jnp.einsum('hqk,khd->qhd', weights.astype(jnp.float32), vh)
        pieces.append(mixed.astype(jnp.bfloat16).reshape(-1, chans))
    return jnp.concatenate(pieces, axis=0)

def attend_all(queries, keys, values, axis):
    count = queries.shape[axis]

    def step(index, result):
        one_q = lax.dynamic_index_in_dim(queries, index, axis, keepdims=False)
        one_k = lax.dynamic_index_in_dim(keys, index, axis, keepdims=False)
        one_v = lax.dynamic_index_in_dim(values, index, axis, keepdims=False)
        mixed = sequence_attention(one_q, one_k, one_v)
        return lax.dynamic_update_index_in_dim(result, mixed, index, axis)
    return lax.fori_loop(0, count, step, jnp.zeros(queries.shape, jnp.bfloat16))

def project(grid, gain, qkv_weight):
    chans = grid.shape[-1]
    normed = layer_norm(grid, gain)
    joined = jnp.dot(normed.reshape(-1, chans), qkv_weight, preferred_element_type=jnp.float32).astype(jnp.bfloat16)
    joined = joined.reshape(grid.shape[:-1] + (3 * chans,))
    return (joined[..., :chans], joined[..., chans:2 * chans], joined[..., 2 * chans:])

def finish(grid, mixed, out_weight):
    chans = grid.shape[-1]
    update = jnp.dot(mixed.reshape(-1, chans), out_weight, preferred_element_type=jnp.float32).reshape(grid.shape)
    return (grid.astype(jnp.float32) + update).astype(jnp.bfloat16)

def attention_branch(grid, gain, qkv_weight, out_weight, axis):
    queries, keys, values = project(grid, gain, qkv_weight)
    mixed = attend_all(queries, keys, values, axis)
    return finish(grid, mixed, out_weight)

def reference(radar_input, conv_weight, conv_bias, row_gain, row_qkv, row_out, col_gain, col_qkv, col_out):
    padded = jnp.pad(radar_input, ((1, 1), (1, 1), (0, 0)))
    hidden = convolve(padded, radar_input, conv_weight, conv_bias)
    second = attention_branch(hidden, row_gain, row_qkv, row_out, 0)
    return attention_branch(second, col_gain, col_qkv, col_out, 1)
```

```python
import functools

import jax
import jax.numpy as jnp
from jax import lax
from jax.experimental import pallas as pl
from jax.experimental.pallas import tpu as pltpu
from jax.sharding import PartitionSpec as P

HEADS = 8
WIDTH = 32
C = 256
SCORE_SCALE = 1.4426950408889634 / 32**0.5
SAFE_SQUARE = 62.0**2
VMEM_LIMIT = 56 * 2**20
F32 = jnp.float32
BF16 = jnp.bfloat16


def dot(a, b):
    return jnp.dot(a, b, preferred_element_type=F32)


def dot_nt(a, b):
    return lax.dot_general(a, b, (((1,), (1,)), ((), ())), preferred_element_type=F32)


def dot_tn(a, b):
    return lax.dot_general(a, b, (((0,), (0,)), ((), ())), preferred_element_type=F32)


def normalize(values, gain):
    center = jnp.mean(values, axis=-1, keepdims=True)
    shifted = values - center
    spread = jnp.mean(shifted * shifted, axis=-1, keepdims=True)
    return (shifted * lax.rsqrt(spread + 1e-05) * gain).astype(BF16)


def projections(normed, wq_t, wk, wv_t, k_ref, qt_ref, vt_ref):
    keys = dot(normed, wk)
    k_ref[...] = keys.astype(BF16)
    queries = dot_nt(wq_t, normed) * SCORE_SCALE
    qt_ref[...] = queries.astype(BF16)
    vt_ref[...] = dot_nt(wv_t, normed).astype(BF16)
    length = normed.shape[0]
    q_norms = jnp.sum((queries * queries).reshape(HEADS, WIDTH, length), axis=1)
    head_of = lax.broadcasted_iota(jnp.int32, (C, 128), 0) // WIDTH
    column = lax.broadcasted_iota(jnp.int32, (C, 128), 1)
    pick = jnp.where(head_of == column, 1.0, 0.0).astype(BF16)
    k_norms = dot((keys * keys).astype(BF16), pick)
    return jnp.max(q_norms) * jnp.max(k_norms) <= SAFE_SQUARE


def attend(safe, k_ref, qt_ref, vt_ref, att_ref, length, tile):
    ones = jnp.ones((16, length), BF16)

    def head_rows(head):
        return slice(head * WIDTH, (head + 1) * WIDTH)

    def finish(mixed):
        return (mixed[:WIDTH] / mixed[WIDTH : WIDTH + 1]).astype(BF16)

    @pl.when(safe)
    def _():
        def step(t, carry):
            cols = pl.ds(pl.multiple_of(t * tile, tile), tile)
            for head in range(HEADS):
                rows = head_rows(head)
                values = jnp.concatenate([vt_ref[rows, :], ones], axis=0)
                scores = dot(k_ref[:, rows], qt_ref[rows, cols])
                expo = jnp.exp2(scores).astype(BF16)
                att_ref[rows, cols] = finish(dot(values, expo))
            return carry

        lax.fori_loop(0, length // tile, step, 0)

    @pl.when(jnp.logical_not(safe))
    def _():
        def step(t, carry):
            cols = pl.ds(pl.multiple_of(t * 256, 256), 256)
            for head in range(HEADS):
                rows = head_rows(head)
                values = jnp.concatenate([vt_ref[rows, :], ones], axis=0)
                scores = dot(k_ref[:, rows], qt_ref[rows, cols])
                expo = jnp.exp2(scores - jnp.max(scores, axis=0, keepdims=True)).astype(BF16)
                att_ref[rows, cols] = finish(dot(values, expo))
            return carry

        lax.fori_loop(0, length // 256, step, 0)


def row_kernel(
    edges, halo, center, inner, wconv, bias, gain, wq_t, wk, wv_t, wout, out_ref,
    taps, hidden, normed, k_ref, qt_ref, vt_ref, att_ref, first,
):
    index = pl.program_id(0)
    length = hidden.shape[0]
    above = 2 * index if edges else 0
    flat = (length, C)
    taps[0:8, :] = jnp.zeros((8, 3 * C), F32)
    taps[length + 8 : length + 16, :] = jnp.zeros((8, 3 * C), F32)
    part = 256
    per = part // center.shape[1]
    for start in range(0, length, part):
        src = slice(start // center.shape[1], start // center.shape[1] + per)
        total = dot(halo[src].reshape(part, C), wconv[above])
        total = total + dot(center[src].reshape(part, C), wconv[1])
        total = total + dot(inner[src].reshape(part, C), wconv[2 - above])
        taps[8 + start : 8 + start + part, :] = total
    for start in range(0, length, part):
        src = slice(start // center.shape[1], start // center.shape[1] + per)
        at = 8 + start
        pre = (
            taps[at - 1 : at - 1 + part, 0:C]
            + taps[at : at + part, C : 2 * C]
            + taps[at + 1 : at + 1 + part, 2 * C : 3 * C]
            + bias[...]
        )
        h = (center[src].reshape(part, C).astype(F32) + jax.nn.gelu(pre)).astype(BF16)
        hidden[start : start + part, :] = h
        normed[start : start + part, :] = normalize(h.astype(F32), gain[...])
    safe = projections(normed[...], wq_t[...], wk[...], wv_t[...], k_ref, qt_ref, vt_ref)
    attend(safe, k_ref, qt_ref, vt_ref, att_ref, length, 512)
    result = hidden[...].astype(F32) + dot_tn(att_ref[...], wout[...])

    @pl.when(index == 0)
    def _():
        first[...] = result

    @pl.when(index == 1)
    def _():
        pair = [first[...].reshape(length // 8, 8, C), result.reshape(length // 8, 8, C)]
        out_ref[...] = jnp.concatenate(pair, axis=1).astype(BF16)


def whole(shape):
    return pl.BlockSpec(shape, lambda i: (0,) * len(shape))


def row_call(edges, halo, rows, wconv, bias, gain, wq_t, wk, wv_t, wout):
    devices, _, cols, _ = rows.shape
    length = devices * cols
    block = (devices, None, cols, C)
    if edges:
        maps = (lambda i: (0, i, 0, 0), lambda i: (0, 3 * i, 0, 0), lambda i: (0, 1 + i, 0, 0))
    else:
        maps = (lambda i: (0, i, 0, 0), lambda i: (0, i + 1, 0, 0), lambda i: (0, i + 2, 0, 0))
    weights = [wconv, bias, gain, wq_t, wk, wv_t, wout]
    flops = 2 * length * C * (9 * C + 4 * C) * 2 + 2 * 2 * HEADS * length * length * 512
    return pl.pallas_call(
        functools.partial(row_kernel, edges),
        grid=(2,),
        in_specs=[pl.BlockSpec(block, m) for m in maps] + [whole(w.shape) for w in weights],
        out_specs=whole((length // 8, 16, C)),
        out_shape=jax.ShapeDtypeStruct((length // 8, 16, C), BF16),
        scratch_shapes=[
            pltpu.VMEM((length + 16, 3 * C), F32),
            pltpu.VMEM((length, C), BF16),
            pltpu.VMEM((length, C), BF16),
            pltpu.VMEM((length, C), BF16),
            pltpu.VMEM((C, length), BF16),
            pltpu.VMEM((C, length), BF16),
            pltpu.VMEM((C, length), BF16),
            pltpu.VMEM((length, C), F32),
        ],
        cost_estimate=pl.CostEstimate(
            flops=flops, bytes_accessed=8 * length * C, transcendentals=2 * HEADS * length**2
        ),
        compiler_params=pltpu.CompilerParams(vmem_limit_bytes=VMEM_LIMIT),
        name="edge_rows" if edges else "middle_rows",
    )(halo, rows, rows, *weights)


def col_kernel(
    middle, edge, gain, wq_t, wk, wv_t, wout, out_ref,
    left, right, k_ref, qt_ref, vt_ref, att_ref,
):
    index = pl.program_id(0)
    length = k_ref.shape[0]
    groups = length // 4

    @pl.when(index == 0)
    def _():
        mid = middle[...].astype(F32)
        out = edge[...].astype(F32)
        order = [out[:, :8], mid, out[:, 8:]]
        whole_cells = jnp.concatenate(order, axis=1).reshape(8 * length, C)
        left[...] = whole_cells[:, :128]
        right[...] = whole_cells[:, 128:]

    mine = pl.ds(index, length, stride=8)
    column = jnp.concatenate([left[mine, :], right[mine, :]], axis=1)
    normed = normalize(column, gain[...])
    safe = projections(normed, wq_t[...], wk[...], wv_t[...], k_ref, qt_ref, vt_ref)
    attend(safe, k_ref, qt_ref, vt_ref, att_ref, length, 512)
    result = column + dot_tn(att_ref[...], wout[...])
    left[mine, :] = result[:, :128]
    right[mine, :] = result[:, 128:]

    @pl.when(index == 7)
    def _():
        blocks = out_ref.shape[0]
        for half, ref in enumerate((left, right)):
            values = ref[...].reshape(groups // blocks, blocks, 32, 128)
            for block in range(blocks):
                part = values[:, block].reshape(length * 8 // blocks, 128)
                out_ref[block, :, 128 * half : 128 * half + 128] = part.astype(BF16)


def col_call(middle, edge, gain, wq_t, wk, wv_t, wout, blocks):
    length = middle.shape[0] * 4
    weights = [gain, wq_t, wk, wv_t, wout]
    shape = (blocks, length * 8 // blocks, C)
    flops = 8 * (2 * length * C * 4 * C + 2 * 2 * HEADS * length * length * 256)
    return pl.pallas_call(
        col_kernel,
        grid=(8,),
        in_specs=[whole(a.shape) for a in [middle, edge] + weights],
        out_specs=whole(shape),
        out_shape=jax.ShapeDtypeStruct(shape, BF16),
        scratch_shapes=[
            pltpu.VMEM((8 * length, 128), F32),
            pltpu.VMEM((8 * length, 128), F32),
            pltpu.VMEM((length, C), BF16),
            pltpu.VMEM((C, length), BF16),
            pltpu.VMEM((C, length), BF16),
            pltpu.VMEM((C, length), BF16),
        ],
        cost_estimate=pl.CostEstimate(
            flops=flops, bytes_accessed=32 * length * C, transcendentals=8 * HEADS * length**2
        ),
        compiler_params=pltpu.CompilerParams(vmem_limit_bytes=VMEM_LIMIT),
        name="columns",
    )(middle, edge, *weights)


def split_weights(qkv):
    return qkv[:, :C].T, qkv[:, C : 2 * C], qkv[:, 2 * C :].T


def shards(
    radar_input, conv_weight, conv_bias, row_gain, row_qkv, row_out, col_gain, col_qkv, col_out
):
    gy, gx = lax.axis_size("gy"), lax.axis_size("gx")
    height, cols, _ = radar_input.shape
    wconv = conv_weight.transpose(0, 2, 1, 3).reshape(3, C, 3 * C)
    row_weights = (wconv, conv_bias.reshape(1, C), row_gain.reshape(1, C)) + split_weights(row_qkv)
    col_weights = (col_gain.reshape(1, C),) + split_weights(col_qkv)
    rows = radar_input.reshape(gx, height // gx, cols, C)
    rows = lax.all_to_all(rows, "gx", split_axis=0, concat_axis=0, tiled=True)
    count = gy * gx
    up = [(i, i + 1) for i in range(count - 1)]
    down = [(j, i) for i, j in up]
    above = lax.ppermute(rows[:, 3], ("gy", "gx"), up)
    below = lax.ppermute(rows[:, 0], ("gy", "gx"), down)
    middle = row_call(False, rows, rows, *row_weights, row_out)
    halo = jnp.stack([above, below], axis=1)
    edge = row_call(True, halo, rows, *row_weights, row_out)
    middle = lax.all_to_all(middle, ("gx", "gy"), split_axis=0, concat_axis=0, tiled=True)
    edge = lax.all_to_all(edge, ("gx", "gy"), split_axis=0, concat_axis=0, tiled=True)
    result = col_call(middle, edge, *col_weights, col_out, gy)
    result = lax.all_to_all(result, "gy", split_axis=0, concat_axis=0, tiled=True)
    result = result.reshape(gy, height, cols // gy, C).transpose(1, 0, 2, 3)
    return result.reshape(height, cols, C)


def solution(mesh):
    in_specs = (P("gy", "gx", None), P(), P(), P(), P(), P(), P(), P(), P())
    out_specs = P("gy", "gx", None)
    return jax.shard_map(shards, mesh=mesh, in_specs=in_specs, out_specs=out_specs, check_vma=False)
```

```python
import functools

import jax
import jax.numpy as jnp
from jax import lax
from jax.experimental import pallas as pl
from jax.experimental.pallas import tpu as pltpu
from jax.sharding import PartitionSpec as P

HEADS = 8
WIDTH = 32
C = 256
SCORE_SCALE = 1.4426950408889634 / 32**0.5
SAFE_SQUARE = 62.0**2
STARTED = WIDTH + 8
VMEM_LIMIT = 56 * 2**20
F32 = jnp.float32
BF16 = jnp.bfloat16


def dot(a, b):
    return jnp.dot(a, b, preferred_element_type=F32)


def dot_nt(a, b):
    return lax.dot_general(a, b, (((1,), (1,)), ((), ())), preferred_element_type=F32)


def dot_tn(a, b):
    return lax.dot_general(a, b, (((0,), (0,)), ((), ())), preferred_element_type=F32)


def normalize(values, gain):
    center = jnp.mean(values, axis=-1, keepdims=True)
    shifted = values - center
    spread = jnp.mean(shifted * shifted, axis=-1, keepdims=True)
    return (shifted * lax.rsqrt(spread + 1e-05) * gain).astype(BF16)


def project(normed, wq_t, wk, wv_t):
    keys = dot(normed, wk)
    queries = dot_nt(wq_t, normed) * SCORE_SCALE
    values = dot_nt(wv_t, normed)
    q_norms = jnp.sum((queries * queries).reshape(HEADS, WIDTH, normed.shape[0]), axis=1)
    head_of = lax.broadcasted_iota(jnp.int32, (C, 128), 0) // WIDTH
    column = lax.broadcasted_iota(jnp.int32, (C, 128), 1)
    pick = jnp.where(head_of == column, 1.0, 0.0).astype(BF16)
    k_norms = dot((keys * keys).astype(BF16), pick)
    rounded = keys.astype(BF16), queries.astype(BF16), values.astype(BF16)
    return rounded, jnp.max(q_norms), jnp.max(k_norms)


def attend(
    safe, sources, qt_ref, att_ref, count, tile, part, joined, started=None, unfinished=False
):
    length = qt_ref.shape[1] // count

    def channels(head, heads=1):
        return slice(head * WIDTH, (head + heads) * WIDTH)

    def with_ones(vt_ref, head, cells, size, heads=1):
        ones = jnp.ones((16, size), BF16)
        return jnp.concatenate([vt_ref[channels(head, heads), cells], ones], axis=0)

    def finish(mixed):
        return (mixed[:WIDTH] / mixed[WIDTH : WIDTH + 1]).astype(BF16)

    def fast():
        units = [
            (sequence, start, head)
            for sequence in range(count)
            for start in range(0, length, tile)
            for head in range(0, HEADS, joined)
        ]
        pieces = [
            (k_ref, vt_ref, k_ref.shape[0] // count, start)
            for k_ref, vt_ref in (sources if started is None else sources[-1:])
            for start in range(0, k_ref.shape[0] // count, part)
        ]
        zeros = jnp.zeros((WIDTH, tile), BF16)

        def diagonal(unit):
            sequence, start, head = unit
            base = sequence * length + start
            rows = []
            for own in range(joined):
                queries = qt_ref[channels(head + own), base : base + tile]
                row = [queries if own == other else zeros for other in range(joined)]
                rows.append(jnp.concatenate(row, axis=1))
            return jnp.concatenate(rows, axis=0)

        def weigh(unit, queries, piece):
            sequence, _, head = unit
            k_ref, _, size, key = piece
            cells = slice(sequence * size + key, sequence * size + key + part)
            return jnp.exp2(dot(k_ref[cells, channels(head, joined)], queries)).astype(BF16)

        queries = diagonal(units[0])
        weights = [weigh(units[0], queries, piece) for piece in pieces]
        for at, (sequence, start, head) in enumerate(units):
            following, total = [], None
            if at + 1 < len(units):
                queries = diagonal(units[at + 1])
            for piece, weight in zip(pieces, weights):
                if at + 1 < len(units):
                    following.append(weigh(units[at + 1], queries, piece))
                _, vt_ref, size, key = piece
                cells = slice(sequence * size + key, sequence * size + key + part)
                term = dot(with_ones(vt_ref, head, cells, part, joined), weight)
                total = term if total is None else total + term
            base = sequence * length + start
            queried = slice(base, base + tile)
            for own in range(joined):
                cols = slice(own * tile, (own + 1) * tile)
                share = total[channels(own), cols]
                norm = total[joined * WIDTH : joined * WIDTH + 8, cols]
                at_sum = (head + own) * STARTED
                at_norm = at_sum + WIDTH
                if unfinished:
                    att_ref[at_sum:at_norm, queried] = share
                    att_ref[at_norm : at_norm + 8, queried] = norm
                    continue
                if started is not None:
                    share = share + started[at_sum:at_norm, queried]
                    norm = norm + started[at_norm : at_norm + 8, queried]
                att_ref[channels(head + own), queried] = (share / norm[:1]).astype(BF16)
            weights = following

    if unfinished:
        fast()
        return
    pl.when(safe)(fast)

    @pl.when(jnp.logical_not(safe))
    def _():
        tiles = length // 256

        def step(t, carry):
            cols = pl.ds(pl.multiple_of(t * 256, 256), 256)
            for head in range(HEADS):
                queries = qt_ref[channels(head), cols]
                scores, cells = [], []
                for k_ref, _ in sources:
                    size = k_ref.shape[0] // count
                    cells.append(pl.ds(pl.multiple_of(t // tiles * size, size), size))
                    scores.append(dot(k_ref[cells[-1], channels(head)], queries))
                tops = [jnp.max(score, axis=0, keepdims=True) for score in scores]
                top = functools.reduce(jnp.maximum, tops)
                mixed = 0.0
                for (_, vt_ref), score, own in zip(sources, scores, cells):
                    expo = jnp.exp2(score - top).astype(BF16)
                    mixed = mixed + dot(with_ones(vt_ref, head, own, score.shape[0]), expo)
                att_ref[channels(head), cols] = finish(mixed)
            return carry

        lax.fori_loop(0, count * tiles, step, 0)


def row_kernel(
    edges, halo_rows, rows, wconv, bias, gain, wq_t, wk, wv_t, wout, out_ref,
    taps, hidden, normed, k_ref, qt_ref, vt_ref, att_ref, first,
):
    index = pl.program_id(0)
    length = hidden.shape[0]
    part = 256
    above = 2 * index if edges else 0
    if edges:
        at_rows = 3 * index, 1 + index
    else:
        at_rows = 1 + index, 2 + index

    def cells(ref, row, start):
        cols = ref.shape[2]
        return ref[start // cols : (start + part) // cols, row].reshape(part, C)

    flat = (length, C)
    taps[0:8, :] = jnp.zeros((8, 3 * C), F32)
    taps[length + 8 : length + 16, :] = jnp.zeros((8, 3 * C), F32)
    weights = jnp.concatenate([wconv[above], wconv[1], wconv[2 - above]], axis=0)
    for start in range(0, length, part):
        around = [cells(halo_rows, index, start)] + [cells(rows, row, start) for row in at_rows]
        total = dot(jnp.concatenate(around, axis=1), weights)
        taps[8 + start : 8 + start + part, :] = total
    for start in range(0, length, part):
        at = 8 + start
        pre = (
            taps[at - 1 : at - 1 + part, 0:C]
            + taps[at : at + part, C : 2 * C]
            + taps[at + 1 : at + 1 + part, 2 * C : 3 * C]
            + bias[...]
        )
        h = (cells(rows, at_rows[0], start).astype(F32) + jax.nn.gelu(pre)).astype(BF16)
        hidden[start : start + part, :] = h
        normed[start : start + part, :] = normalize(h.astype(F32), gain[...])
    rounded, q_square, k_square = project(normed[...], wq_t[...], wk[...], wv_t[...])
    k_ref[...], qt_ref[...], vt_ref[...] = rounded
    safe = q_square * k_square <= SAFE_SQUARE
    attend(safe, [(k_ref, vt_ref)], qt_ref, att_ref, 1, 512, 256, 1)
    result = hidden[...].astype(F32) + dot_tn(att_ref[...], wout[...])

    @pl.when(index == 0)
    def _():
        first[...] = result

    @pl.when(index == 1)
    def _():
        pair = [first[...].reshape(length // 8, 8, C), result.reshape(length // 8, 8, C)]
        out_ref[...] = jnp.concatenate(pair, axis=1).astype(BF16)


def whole(shape):
    return pl.BlockSpec(shape, lambda i: (0,) * len(shape))


def row_call(edges, halo, rows, wconv, bias, gain, wq_t, wk, wv_t, wout):
    devices, _, cols, _ = rows.shape
    length = devices * cols
    weights = [wconv, bias, gain, wq_t, wk, wv_t, wout]
    flops = 2 * length * C * (9 * C + 4 * C) * 2 + 2 * 2 * HEADS * length * length * 512
    return pl.pallas_call(
        functools.partial(row_kernel, edges),
        grid=(2,),
        in_specs=[pl.BlockSpec(memory_space=pltpu.VMEM)] * (2 + len(weights)),
        out_specs=whole((length // 8, 16, C)),
        out_shape=jax.ShapeDtypeStruct((length // 8, 16, C), BF16),
        scratch_shapes=[
            pltpu.VMEM((length + 16, 3 * C), F32),
            pltpu.VMEM((length, C), BF16),
            pltpu.VMEM((length, C), BF16),
            pltpu.VMEM((length, C), BF16),
            pltpu.VMEM((C, length), BF16),
            pltpu.VMEM((C, length), BF16),
            pltpu.VMEM((C, length), BF16),
            pltpu.VMEM((length, C), F32),
        ],
        cost_estimate=pl.CostEstimate(
            flops=flops, bytes_accessed=8 * length * C, transcendentals=2 * HEADS * length**2
        ),
        compiler_params=pltpu.CompilerParams(vmem_limit_bytes=36 * 2**20),
        name="edge_rows" if edges else "middle_rows",
    )(halo, rows, *weights)


def load_cells(block, left, right):
    cells = block[...].astype(F32).reshape(left.shape[0], C)
    left[...] = cells[:, :128]
    right[...] = cells[:, 128:]


def two_columns(index, length):
    return [pl.ds(2 * index + side, length, stride=8) for side in range(2)]


def project_columns(left, right, gain, wq_t, wk, wv_t, x_ref, k_ref, qt_ref, vt_ref, norms):
    index = pl.program_id(0)
    length = x_ref.shape[0] // 2
    columns = jnp.concatenate(
        [
            jnp.concatenate([left[cells, :], right[cells, :]], axis=1)
            for cells in two_columns(index, length)
        ],
        axis=0,
    )
    x_ref[...] = columns.astype(BF16)
    normed = normalize(columns, gain[...])
    rounded, q_square, k_square = project(normed, wq_t[...], wk[...], wv_t[...])
    k_ref[...], qt_ref[...], vt_ref[...] = rounded

    @pl.when(index == 0)
    def _():
        norms[...] = jnp.zeros(norms.shape, F32)

    norms[0] = jnp.maximum(norms[0], q_square)
    norms[1] = jnp.maximum(norms[1], k_square)


def attend_columns(
    norms, sources, qt_ref, x_ref, wout, att_ref, left, right, out_ref, started=None
):
    index = pl.program_id(0)
    length = x_ref.shape[0] // 2
    q_square, k_squares = jnp.max(norms[0][0]), [jnp.max(norm[1]) for norm in norms]
    safe = q_square * functools.reduce(jnp.maximum, k_squares) <= SAFE_SQUARE
    attend(safe, sources, qt_ref, att_ref, 2, 256, 256, 2, started)
    result = x_ref[...].astype(F32) + dot_tn(att_ref[...], wout[...])
    for side, cells in enumerate(two_columns(index, length)):
        left[cells, :] = result[side * length : (side + 1) * length, :128]
        right[cells, :] = result[side * length : (side + 1) * length, 128:]

    @pl.when(index == 3)
    def _():
        blocks, size, _ = out_ref.shape
        for half, ref in enumerate((left, right)):
            values = ref[...].reshape(size // 16, blocks, 16, 128)
            for block in range(blocks):
                part = values[:, block].reshape(size, 128)
                out_ref[block, :, 128 * half : 128 * half + 128] = part.astype(BF16)


def first_kernel(
    block, gain, wq_t, wk, wv_t, x_ref, k_ref, qt_ref, vt_ref, norms, sums, left, right
):
    @pl.when(pl.program_id(0) == 0)
    def _():
        load_cells(block, left, right)

    project_columns(left, right, gain, wq_t, wk, wv_t, x_ref, k_ref, qt_ref, vt_ref, norms)
    attend(None, [(k_ref, vt_ref)], qt_ref, sums, 2, 256, 256, 2, unfinished=True)


def second_kernel(
    block, gain, wq_t, wk, wv_t, wout, xa_ref, ka_ref, qta_ref, vta_ref, norms_a, sums,
    out_ref, x_ref, k_ref, qt_ref, vt_ref, norms, left, right, left_out, right_out, att_ref,
):
    @pl.when(pl.program_id(0) == 0)
    def _():
        load_cells(block, left, right)

    project_columns(left, right, gain, wq_t, wk, wv_t, x_ref, k_ref, qt_ref, vt_ref, norms)
    sources = [(ka_ref, vta_ref), (k_ref, vt_ref)]
    attend_columns(
        [norms_a, norms], sources, qta_ref, xa_ref, wout, att_ref, left_out, right_out, out_ref, sums
    )


def third_kernel(
    wout, ka_ref, vta_ref, norms_a, x_ref, k_ref, qt_ref, vt_ref, norms, out_ref,
    left, right, att_ref,
):
    sources = [(ka_ref, vta_ref), (k_ref, vt_ref)]
    attend_columns([norms, norms_a], sources, qt_ref, x_ref, wout, att_ref, left, right, out_ref)


def col_calls(gain, wq_t, wk, wv_t, wout, blocks):
    def calls(cells):
        pair = cells // 4
        spec_x = pl.BlockSpec((pair, C), lambda i: (i, 0))
        spec_t = pl.BlockSpec((C, pair), lambda i: (0, i))
        spec_n = whole((2, 8, 128))
        spec_s = pl.BlockSpec((HEADS * STARTED, pair), lambda i: (0, i))
        sums_shape = jax.ShapeDtypeStruct((HEADS * STARTED, cells), F32)
        part_specs = [spec_x, spec_x, spec_t, spec_t, spec_n]
        part_shapes = [
            jax.ShapeDtypeStruct((cells, C), BF16),
            jax.ShapeDtypeStruct((cells, C), BF16),
            jax.ShapeDtypeStruct((C, cells), BF16),
            jax.ShapeDtypeStruct((C, cells), BF16),
            jax.ShapeDtypeStruct((2, 8, 128), F32),
        ]
        out = (blocks, cells // blocks, C)
        out_shape = jax.ShapeDtypeStruct(out, BF16)
        halves = [pltpu.VMEM((cells, 128), F32)] * 2
        att = pltpu.VMEM((C, pair), BF16)
        project_flops = 2 * cells * C * 3 * C
        attend_flops = 2 * 2 * HEADS * cells * (cells // 4) * 256 + 2 * cells * C * C

        def call(kernel, name, args, in_specs, out_specs, out_shapes, scratch, flops, exps):
            return pl.pallas_call(
                kernel,
                grid=(4,),
                in_specs=in_specs,
                out_specs=out_specs,
                out_shape=out_shapes,
                scratch_shapes=scratch,
                cost_estimate=pl.CostEstimate(
                    flops=flops, bytes_accessed=8 * cells * C, transcendentals=exps
                ),
                compiler_params=pltpu.CompilerParams(vmem_limit_bytes=VMEM_LIMIT),
                name=name,
            )(*args)

        weights = [gain, wq_t, wk, wv_t]
        weight_specs = [whole(w.shape) for w in weights]
        wout_spec = whole(wout.shape)
        exps = HEADS * cells * cells // 4

        def first(block):
            return call(
                first_kernel, "first_projections", [block] + weights,
                [whole(block.shape)] + weight_specs, part_specs + [spec_s],
                part_shapes + [sums_shape], halves, project_flops + attend_flops // 2, exps // 2,
            )

        def second(block, part):
            results = call(
                second_kernel, "first_queries", [block] + weights + [wout] + list(part),
                [whole(block.shape)] + weight_specs + [wout_spec] + part_specs + [spec_s],
                [whole(out)] + part_specs, [out_shape] + part_shapes, halves * 2 + [att],
                project_flops + attend_flops // 2, exps // 2,
            )
            return results[0], results[1:]

        def third(part, other):
            return call(
                third_kernel, "second_queries",
                [wout, part[1], part[3], part[4]] + list(other),
                [wout_spec, spec_x, spec_t, spec_n] + part_specs, whole(out), out_shape,
                halves + [att], attend_flops, exps,
            )

        return first, second, third

    return calls


def split_weights(qkv):
    return qkv[:, :C].T, qkv[:, C : 2 * C], qkv[:, 2 * C :].T


def shards(
    radar_input, conv_weight, conv_bias, row_gain, row_qkv, row_out, col_gain, col_qkv, col_out
):
    gy, gx = lax.axis_size("gy"), lax.axis_size("gx")
    height, cols, _ = radar_input.shape
    wconv = conv_weight.transpose(0, 2, 1, 3).reshape(3, C, 3 * C)
    row_weights = (wconv, conv_bias.reshape(1, C), row_gain.reshape(1, C)) + split_weights(row_qkv)
    col_weights = (col_gain.reshape(1, C),) + split_weights(col_qkv)
    rows = radar_input.reshape(gx, height // gx, cols, C)
    rows = lax.all_to_all(rows, "gx", split_axis=0, concat_axis=0, tiled=True)
    count = gy * gx
    up = [(i, i + 1) for i in range(count - 1)]
    down = [(j, i) for i, j in up]
    above = lax.ppermute(rows[:, 3], ("gy", "gx"), up)
    below = lax.ppermute(rows[:, 0], ("gy", "gx"), down)
    middle = row_call(False, rows, rows, *row_weights, row_out)
    halo = jnp.stack([above, below], axis=1)
    edge = row_call(True, halo, rows, *row_weights, row_out)
    middle = lax.all_to_all(middle, ("gx", "gy"), split_axis=0, concat_axis=0, tiled=True)
    first, second, third = col_calls(*col_weights, col_out, gy)(middle.shape[0] * 16)
    part = first(middle)
    edge = lax.all_to_all(edge, ("gx", "gy"), split_axis=0, concat_axis=0, tiled=True)
    middle, other = second(edge, part)
    middle = lax.all_to_all(middle, "gy", split_axis=0, concat_axis=0, tiled=True)
    edge, middle = lax.optimization_barrier((third(part, other), middle))
    edge = lax.all_to_all(edge, "gy", split_axis=0, concat_axis=0, tiled=True)
    middle, edge = (
        rows.reshape(gy, height // 4, 2, cols // gy, C).transpose(1, 2, 0, 3, 4)
        for rows in (middle, edge)
    )
    result = jnp.concatenate([edge[:, :1], middle, edge[:, 1:]], axis=1)
    return result.reshape(height, cols, C)


def solution(mesh):
    in_specs = (P("gy", "gx", None), P(), P(), P(), P(), P(), P(), P(), P())
    out_specs = P("gy", "gx", None)
    return jax.shard_map(shards, mesh=mesh, in_specs=in_specs, out_specs=out_specs, check_vma=False)
```

```python
import functools

import jax
import jax.numpy as jnp
from jax import lax
from jax.experimental import pallas as pl
from jax.experimental.pallas import tpu as pltpu
from jax.sharding import PartitionSpec as P

HEADS = 8
WIDTH = 32
C = 256
SCORE_SCALE = 1.4426950408889634 / 32**0.5
SAFE_SQUARE = 62.0**2
STARTED = WIDTH + 8
VMEM_LIMIT = 56 * 2**20
F32 = jnp.float32
BF16 = jnp.bfloat16


def dot(a, b):
    return jnp.dot(a, b, preferred_element_type=F32)


def dot_nt(a, b):
    return lax.dot_general(a, b, (((1,), (1,)), ((), ())), preferred_element_type=F32)


def dot_tn(a, b):
    return lax.dot_general(a, b, (((0,), (0,)), ((), ())), preferred_element_type=F32)


def normalize(values, gain):
    center = jnp.mean(values, axis=-1, keepdims=True)
    shifted = values - center
    spread = jnp.mean(shifted * shifted, axis=-1, keepdims=True)
    return (shifted * lax.rsqrt(spread + 1e-05) * gain).astype(BF16)


def project(normed, wq_t, wk, wv_t):
    keys = dot(normed, wk)
    queries = dot_nt(wq_t, normed) * SCORE_SCALE
    values = dot_nt(wv_t, normed)
    q_norms = jnp.sum((queries * queries).reshape(HEADS, WIDTH, normed.shape[0]), axis=1)
    head_of = lax.broadcasted_iota(jnp.int32, (C, 128), 0) // WIDTH
    column = lax.broadcasted_iota(jnp.int32, (C, 128), 1)
    pick = jnp.where(head_of == column, 1.0, 0.0).astype(BF16)
    k_norms = dot((keys * keys).astype(BF16), pick)
    rounded = keys.astype(BF16), queries.astype(BF16), values.astype(BF16)
    return rounded, jnp.max(q_norms), jnp.max(k_norms)


def attend(
    safe, sources, qt_ref, att_ref, count, tile, part, joined, started=None, unfinished=False
):
    length = qt_ref.shape[1] // count

    def channels(head, heads=1):
        return slice(head * WIDTH, (head + heads) * WIDTH)

    def with_ones(vt_ref, head, cells, size, heads=1):
        ones = jnp.ones((16, size), BF16)
        return jnp.concatenate([vt_ref[channels(head, heads), cells], ones], axis=0)

    def fast():
        units = [
            (sequence, start, head)
            for sequence in range(count)
            for start in range(0, length, tile)
            for head in range(0, HEADS, joined)
        ]
        pieces = [
            (k_ref, vt_ref, k_ref.shape[0] // count, start)
            for k_ref, vt_ref in (sources if started is None else sources[-1:])
            for start in range(0, k_ref.shape[0] // count, part)
        ]
        zeros = jnp.zeros((WIDTH, tile), BF16)

        def diagonal(unit):
            sequence, start, head = unit
            base = sequence * length + start
            rows = []
            for own in range(joined):
                queries = qt_ref[channels(head + own), base : base + tile]
                row = [queries if own == other else zeros for other in range(joined)]
                rows.append(jnp.concatenate(row, axis=1))
            return jnp.concatenate(rows, axis=0)

        def weigh(unit, queries, piece):
            sequence, _, head = unit
            k_ref, _, size, key = piece
            cells = slice(sequence * size + key, sequence * size + key + part)
            return jnp.exp2(dot(k_ref[cells, channels(head, joined)], queries)).astype(BF16)

        queries = diagonal(units[0])
        weights = [weigh(units[0], queries, piece) for piece in pieces]
        for at, (sequence, start, head) in enumerate(units):
            following, total = [], None
            if at + 1 < len(units):
                queries = diagonal(units[at + 1])
            for piece, weight in zip(pieces, weights):
                if at + 1 < len(units):
                    following.append(weigh(units[at + 1], queries, piece))
                _, vt_ref, size, key = piece
                cells = slice(sequence * size + key, sequence * size + key + part)
                term = dot(with_ones(vt_ref, head, cells, part, joined), weight)
                total = term if total is None else total + term
            base = sequence * length + start
            queried = slice(base, base + tile)
            for own in range(joined):
                cols = slice(own * tile, (own + 1) * tile)
                share = total[channels(own), cols]
                norm = total[joined * WIDTH : joined * WIDTH + 8, cols]
                at_sum = (head + own) * STARTED
                at_norm = at_sum + WIDTH
                if unfinished:
                    att_ref[at_sum:at_norm, queried] = share
                    att_ref[at_norm : at_norm + 8, queried] = norm
                    continue
                if started is not None:
                    share = share + started[at_sum:at_norm, queried]
                    norm = norm + started[at_norm : at_norm + 8, queried]
                att_ref[channels(head + own), queried] = (share / norm[:1]).astype(BF16)
            weights = following

    if unfinished:
        fast()
        return
    pl.when(safe)(fast)

    @pl.when(jnp.logical_not(safe))
    def _():
        tiles = length // 256

        def step(t, carry):
            head = t % HEADS
            index = t // HEADS
            cols = pl.ds(pl.multiple_of(index * 256, 256), 256)
            rows = pl.ds(pl.multiple_of(head * WIDTH, WIDTH), WIDTH)
            owner = lax.broadcasted_iota(jnp.int32, (C, 256), 0) // WIDTH
            queries = jnp.where(owner == head, qt_ref[:, cols], jnp.zeros((C, 256), BF16))
            scores, owns = [], []
            for k_ref, _ in sources:
                size = k_ref.shape[0] // count
                owns.append(pl.ds(pl.multiple_of(index // tiles * size, size), size))
                scores.append(dot(k_ref[owns[-1], :], queries))
            tops = [jnp.max(score, axis=0, keepdims=True) for score in scores]
            top = functools.reduce(jnp.maximum, tops)
            mixed = 0.0
            for (_, vt_ref), score, own in zip(sources, scores, owns):
                expo = jnp.exp2(score - top).astype(BF16)
                ones = jnp.ones((16, score.shape[0]), BF16)
                mixed = mixed + dot(jnp.concatenate([vt_ref[rows, own], ones], axis=0), expo)
            att_ref[rows, cols] = (mixed[:WIDTH] / mixed[WIDTH : WIDTH + 1]).astype(BF16)
            return carry

        lax.fori_loop(0, count * tiles * HEADS, step, 0)


def row_kernel(
    edges, halo_rows, rows, wconv, bias, gain, wq_t, wk, wv_t, wout, out_ref,
    taps, hidden, normed, k_ref, qt_ref, vt_ref, att_ref, first,
):
    index = pl.program_id(0)
    length = hidden.shape[0]
    part = 256
    above = 2 * index if edges else 0
    if edges:
        at_rows = 3 * index, 1 + index
    else:
        at_rows = 1 + index, 2 + index

    def cells(ref, row, start):
        cols = ref.shape[2]
        return ref[start // cols : (start + part) // cols, row].reshape(part, C)

    flat = (length, C)
    taps[0:8, :] = jnp.zeros((8, 3 * C), F32)
    taps[length + 8 : length + 16, :] = jnp.zeros((8, 3 * C), F32)
    weights = jnp.concatenate([wconv[above], wconv[1], wconv[2 - above]], axis=0)
    for start in range(0, length, part):
        around = [cells(halo_rows, index, start)] + [cells(rows, row, start) for row in at_rows]
        total = dot(jnp.concatenate(around, axis=1), weights)
        taps[8 + start : 8 + start + part, :] = total
    for start in range(0, length, part):
        at = 8 + start
        pre = (
            taps[at - 1 : at - 1 + part, 0:C]
            + taps[at : at + part, C : 2 * C]
            + taps[at + 1 : at + 1 + part, 2 * C : 3 * C]
            + bias[...]
        )
        h = (cells(rows, at_rows[0], start).astype(F32) + jax.nn.gelu(pre)).astype(BF16)
        hidden[start : start + part, :] = h
        normed[start : start + part, :] = normalize(h.astype(F32), gain[...])
    rounded, q_square, k_square = project(normed[...], wq_t[...], wk[...], wv_t[...])
    k_ref[...], qt_ref[...], vt_ref[...] = rounded
    safe = q_square * k_square <= SAFE_SQUARE
    attend(safe, [(k_ref, vt_ref)], qt_ref, att_ref, 1, 512, 256, 1)
    result = hidden[...].astype(F32) + dot_tn(att_ref[...], wout[...])

    @pl.when(index == 0)
    def _():
        first[...] = result

    @pl.when(index == 1)
    def _():
        pair = [first[...].reshape(length // 8, 8, C), result.reshape(length // 8, 8, C)]
        out_ref[...] = jnp.concatenate(pair, axis=1).astype(BF16)


def whole(shape):
    return pl.BlockSpec(shape, lambda i: (0,) * len(shape))


def row_call(edges, halo, rows, wconv, bias, gain, wq_t, wk, wv_t, wout):
    devices, _, cols, _ = rows.shape
    length = devices * cols
    weights = [wconv, bias, gain, wq_t, wk, wv_t, wout]
    flops = 2 * length * C * (9 * C + 4 * C) * 2 + 2 * 2 * HEADS * length * length * 512
    return pl.pallas_call(
        functools.partial(row_kernel, edges),
        grid=(2,),
        in_specs=[pl.BlockSpec(memory_space=pltpu.VMEM)] * (2 + len(weights)),
        out_specs=whole((length // 8, 16, C)),
        out_shape=jax.ShapeDtypeStruct((length // 8, 16, C), BF16),
        scratch_shapes=[
            pltpu.VMEM((length + 16, 3 * C), F32),
            pltpu.VMEM((length, C), BF16),
            pltpu.VMEM((length, C), BF16),
            pltpu.VMEM((length, C), BF16),
            pltpu.VMEM((C, length), BF16),
            pltpu.VMEM((C, length), BF16),
            pltpu.VMEM((C, length), BF16),
            pltpu.VMEM((length, C), F32),
        ],
        cost_estimate=pl.CostEstimate(
            flops=flops, bytes_accessed=8 * length * C, transcendentals=2 * HEADS * length**2
        ),
        compiler_params=pltpu.CompilerParams(vmem_limit_bytes=36 * 2**20),
        name="edge_rows" if edges else "middle_rows",
    )(halo, rows, *weights)


def load_cells(block, left, right):
    cells = block[...].astype(F32).reshape(left.shape[0], C)
    left[...] = cells[:, :128]
    right[...] = cells[:, 128:]


def two_columns(index, length):
    return [pl.ds(2 * index + side, length, stride=8) for side in range(2)]


def project_columns(left, right, gain, wq_t, wk, wv_t, x_ref, k_ref, qt_ref, vt_ref, norms):
    index = pl.program_id(0)
    length = x_ref.shape[0] // 2
    columns = jnp.concatenate(
        [
            jnp.concatenate([left[cells, :], right[cells, :]], axis=1)
            for cells in two_columns(index, length)
        ],
        axis=0,
    )
    x_ref[...] = columns.astype(BF16)
    normed = normalize(columns, gain[...])
    rounded, q_square, k_square = project(normed, wq_t[...], wk[...], wv_t[...])
    k_ref[...], qt_ref[...], vt_ref[...] = rounded

    @pl.when(index == 0)
    def _():
        norms[...] = jnp.zeros(norms.shape, F32)

    norms[0] = jnp.maximum(norms[0], q_square)
    norms[1] = jnp.maximum(norms[1], k_square)


def attend_columns(
    norms, sources, qt_ref, x_ref, wout, att_ref, left, right, out_ref, started=None
):
    index = pl.program_id(0)
    length = x_ref.shape[0] // 2
    q_square, k_squares = jnp.max(norms[0][0]), [jnp.max(norm[1]) for norm in norms]
    safe = q_square * functools.reduce(jnp.maximum, k_squares) <= SAFE_SQUARE
    attend(safe, sources, qt_ref, att_ref, 2, 256, 256, 2, started)
    result = x_ref[...].astype(F32) + dot_tn(att_ref[...], wout[...])
    for side, cells in enumerate(two_columns(index, length)):
        left[cells, :] = result[side * length : (side + 1) * length, :128]
        right[cells, :] = result[side * length : (side + 1) * length, 128:]

    @pl.when(index == 3)
    def _():
        blocks, size, _ = out_ref.shape
        for half, ref in enumerate((left, right)):
            values = ref[...].reshape(size // 16, blocks, 16, 128)
            for block in range(blocks):
                part = values[:, block].reshape(size, 128)
                out_ref[block, :, 128 * half : 128 * half + 128] = part.astype(BF16)


def first_kernel(
    block, gain, wq_t, wk, wv_t, x_ref, k_ref, qt_ref, vt_ref, norms, sums, left, right
):
    @pl.when(pl.program_id(0) == 0)
    def _():
        load_cells(block, left, right)

    project_columns(left, right, gain, wq_t, wk, wv_t, x_ref, k_ref, qt_ref, vt_ref, norms)
    attend(None, [(k_ref, vt_ref)], qt_ref, sums, 2, 256, 256, 2, unfinished=True)


def second_kernel(
    block, gain, wq_t, wk, wv_t, wout, xa_ref, ka_ref, qta_ref, vta_ref, norms_a, sums,
    out_ref, x_ref, k_ref, qt_ref, vt_ref, norms, left, right, left_out, right_out, att_ref,
):
    @pl.when(pl.program_id(0) == 0)
    def _():
        load_cells(block, left, right)

    project_columns(left, right, gain, wq_t, wk, wv_t, x_ref, k_ref, qt_ref, vt_ref, norms)
    sources = [(ka_ref, vta_ref), (k_ref, vt_ref)]
    attend_columns(
        [norms_a, norms], sources, qta_ref, xa_ref, wout, att_ref, left_out, right_out, out_ref, sums
    )


def third_kernel(
    wout, ka_ref, vta_ref, norms_a, x_ref, k_ref, qt_ref, vt_ref, norms, out_ref,
    left, right, att_ref,
):
    sources = [(ka_ref, vta_ref), (k_ref, vt_ref)]
    attend_columns([norms, norms_a], sources, qt_ref, x_ref, wout, att_ref, left, right, out_ref)


def col_calls(gain, wq_t, wk, wv_t, wout, blocks):
    def calls(cells):
        pair = cells // 4
        spec_x = pl.BlockSpec((pair, C), lambda i: (i, 0))
        spec_t = pl.BlockSpec((C, pair), lambda i: (0, i))
        spec_n = whole((2, 8, 128))
        spec_s = pl.BlockSpec((HEADS * STARTED, pair), lambda i: (0, i))
        sums_shape = jax.ShapeDtypeStruct((HEADS * STARTED, cells), F32)
        part_specs = [spec_x, spec_x, spec_t, spec_t, spec_n]
        part_shapes = [
            jax.ShapeDtypeStruct((cells, C), BF16),
            jax.ShapeDtypeStruct((cells, C), BF16),
            jax.ShapeDtypeStruct((C, cells), BF16),
            jax.ShapeDtypeStruct((C, cells), BF16),
            jax.ShapeDtypeStruct((2, 8, 128), F32),
        ]
        out = (blocks, cells // blocks, C)
        out_shape = jax.ShapeDtypeStruct(out, BF16)
        halves = [pltpu.VMEM((cells, 128), F32)] * 2
        att = pltpu.VMEM((C, pair), BF16)
        project_flops = 2 * cells * C * 3 * C
        attend_flops = 2 * 2 * HEADS * cells * (cells // 4) * 256 + 2 * cells * C * C

        def call(kernel, name, args, in_specs, out_specs, out_shapes, scratch, flops, exps):
            return pl.pallas_call(
                kernel,
                grid=(4,),
                in_specs=in_specs,
                out_specs=out_specs,
                out_shape=out_shapes,
                scratch_shapes=scratch,
                cost_estimate=pl.CostEstimate(
                    flops=flops, bytes_accessed=8 * cells * C, transcendentals=exps
                ),
                compiler_params=pltpu.CompilerParams(vmem_limit_bytes=VMEM_LIMIT),
                name=name,
            )(*args)

        weights = [gain, wq_t, wk, wv_t]
        weight_specs = [whole(w.shape) for w in weights]
        wout_spec = whole(wout.shape)
        exps = HEADS * cells * cells // 4

        def first(block):
            return call(
                first_kernel, "first_projections", [block] + weights,
                [whole(block.shape)] + weight_specs, part_specs + [spec_s],
                part_shapes + [sums_shape], halves, project_flops + attend_flops // 2, exps // 2,
            )

        def second(block, part):
            results = call(
                second_kernel, "first_queries", [block] + weights + [wout] + list(part),
                [whole(block.shape)] + weight_specs + [wout_spec] + part_specs + [spec_s],
                [whole(out)] + part_specs, [out_shape] + part_shapes, halves * 2 + [att],
                project_flops + attend_flops // 2, exps // 2,
            )
            return results[0], results[1:]

        def third(part, other):
            return call(
                third_kernel, "second_queries",
                [wout, part[1], part[3], part[4]] + list(other),
                [wout_spec, spec_x, spec_t, spec_n] + part_specs, whole(out), out_shape,
                halves + [att], attend_flops, exps,
            )

        return first, second, third

    return calls


def split_weights(qkv):
    return qkv[:, :C].T, qkv[:, C : 2 * C], qkv[:, 2 * C :].T


def shards(
    radar_input, conv_weight, conv_bias, row_gain, row_qkv, row_out, col_gain, col_qkv, col_out
):
    gy, gx = lax.axis_size("gy"), lax.axis_size("gx")
    height, cols, _ = radar_input.shape
    wconv = conv_weight.transpose(0, 2, 1, 3).reshape(3, C, 3 * C)
    row_weights = (wconv, conv_bias.reshape(1, C), row_gain.reshape(1, C)) + split_weights(row_qkv)
    col_weights = (col_gain.reshape(1, C),) + split_weights(col_qkv)
    rows = radar_input.reshape(gx, height // gx, cols, C)
    rows = lax.all_to_all(rows, "gx", split_axis=0, concat_axis=0, tiled=True)
    count = gy * gx
    up = [(i, i + 1) for i in range(count - 1)]
    down = [(j, i) for i, j in up]
    above = lax.ppermute(rows[:, 3], ("gy", "gx"), up)
    below = lax.ppermute(rows[:, 0], ("gy", "gx"), down)
    middle = row_call(False, rows, rows, *row_weights, row_out)
    halo = jnp.stack([above, below], axis=1)
    edge = row_call(True, halo, rows, *row_weights, row_out)
    middle = lax.all_to_all(middle, ("gx", "gy"), split_axis=0, concat_axis=0, tiled=True)
    first, second, third = col_calls(*col_weights, col_out, gy)(middle.shape[0] * 16)
    part = first(middle)
    edge = lax.all_to_all(edge, ("gx", "gy"), split_axis=0, concat_axis=0, tiled=True)
    middle, other = second(edge, part)
    middle = lax.all_to_all(middle, "gy", split_axis=0, concat_axis=0, tiled=True)
    edge, middle = lax.optimization_barrier((third(part, other), middle))
    edge = lax.all_to_all(edge, "gy", split_axis=0, concat_axis=0, tiled=True)
    middle, edge = (
        rows.reshape(gy, height // 4, 2, cols // gy, C).transpose(1, 2, 0, 3, 4)
        for rows in (middle, edge)
    )
    result = jnp.concatenate([edge[:, :1], middle, edge[:, 1:]], axis=1)
    return result.reshape(height, cols, C)


def solution(mesh):
    in_specs = (P("gy", "gx", None), P(), P(), P(), P(), P(), P(), P(), P())
    out_specs = P("gy", "gx", None)
    return jax.shard_map(shards, mesh=mesh, in_specs=in_specs, out_specs=out_specs, check_vma=False)
```

```python
import functools

import jax
import jax.numpy as jnp
from jax import lax
from jax.experimental import pallas as pl
from jax.experimental.pallas import tpu as pltpu
from jax.sharding import PartitionSpec as P

HEADS = 8
WIDTH = 32
C = 256
SCORE_SCALE = 1.4426950408889634 / 32**0.5
SAFE_SQUARE = 62.0**2
STARTED = WIDTH + 8
VMEM_LIMIT = 56 * 2**20
F32 = jnp.float32
BF16 = jnp.bfloat16


def dot(a, b):
    return jnp.dot(a, b, preferred_element_type=F32)


def dot_nt(a, b):
    return lax.dot_general(a, b, (((1,), (1,)), ((), ())), preferred_element_type=F32)


def dot_tn(a, b):
    return lax.dot_general(a, b, (((0,), (0,)), ((), ())), preferred_element_type=F32)


def normalize(values, gain):
    center = jnp.mean(values, axis=-1, keepdims=True)
    shifted = values - center
    spread = jnp.mean(shifted * shifted, axis=-1, keepdims=True)
    return (shifted * lax.rsqrt(spread + 1e-05) * gain).astype(BF16)


def project(normed, wq_t, wk, wv_t):
    keys = dot(normed, wk)
    queries = dot_nt(wq_t, normed) * SCORE_SCALE
    values = dot_nt(wv_t, normed)
    q_norms = jnp.sum((queries * queries).reshape(HEADS, WIDTH, normed.shape[0]), axis=1)
    head_of = lax.broadcasted_iota(jnp.int32, (C, 128), 0) // WIDTH
    column = lax.broadcasted_iota(jnp.int32, (C, 128), 1)
    pick = jnp.where(head_of == column, 1.0, 0.0).astype(BF16)
    k_norms = dot((keys * keys).astype(BF16), pick)
    rounded = keys.astype(BF16), queries.astype(BF16), values.astype(BF16)
    return rounded, jnp.max(q_norms), jnp.max(k_norms)


def attend(
    safe, sources, qt_ref, att_ref, count, tile, part, joined, started=None, unfinished=False
):
    length = qt_ref.shape[1] // count

    def channels(head, heads=1):
        return slice(head * WIDTH, (head + heads) * WIDTH)

    def with_ones(vt_ref, head, cells, size, heads=1):
        ones = jnp.ones((16, size), BF16)
        return jnp.concatenate([vt_ref[channels(head, heads), cells], ones], axis=0)

    def fast():
        units = [
            (sequence, start, head)
            for sequence in range(count)
            for start in range(0, length, tile)
            for head in range(0, HEADS, joined)
        ]
        pieces = [
            (k_ref, vt_ref, k_ref.shape[0] // count, start)
            for k_ref, vt_ref in (sources if started is None else sources[-1:])
            for start in range(0, k_ref.shape[0] // count, part)
        ]
        zeros = jnp.zeros((WIDTH, tile), BF16)

        def diagonal(unit):
            sequence, start, head = unit
            base = sequence * length + start
            rows = []
            for own in range(joined):
                queries = qt_ref[channels(head + own), base : base + tile]
                row = [queries if own == other else zeros for other in range(joined)]
                rows.append(jnp.concatenate(row, axis=1))
            return jnp.concatenate(rows, axis=0)

        def weigh(unit, queries, piece):
            sequence, _, head = unit
            k_ref, _, size, key = piece
            cells = slice(sequence * size + key, sequence * size + key + part)
            return jnp.exp2(dot(k_ref[cells, channels(head, joined)], queries)).astype(BF16)

        queries = diagonal(units[0])
        weights = [weigh(units[0], queries, piece) for piece in pieces]
        for at, (sequence, start, head) in enumerate(units):
            following, total = [], None
            if at + 1 < len(units):
                queries = diagonal(units[at + 1])
            for piece, weight in zip(pieces, weights):
                if at + 1 < len(units):
                    following.append(weigh(units[at + 1], queries, piece))
                _, vt_ref, size, key = piece
                cells = slice(sequence * size + key, sequence * size + key + part)
                term = dot(with_ones(vt_ref, head, cells, part, joined), weight)
                total = term if total is None else total + term
            base = sequence * length + start
            queried = slice(base, base + tile)
            for own in range(joined):
                cols = slice(own * tile, (own + 1) * tile)
                share = total[channels(own), cols]
                norm = total[joined * WIDTH : joined * WIDTH + 8, cols]
                at_sum = (head + own) * STARTED
                at_norm = at_sum + WIDTH
                if unfinished:
                    att_ref[at_sum:at_norm, queried] = share
                    att_ref[at_norm : at_norm + 8, queried] = norm
                    continue
                if started is not None:
                    share = share + started[at_sum:at_norm, queried]
                    norm = norm + started[at_norm : at_norm + 8, queried]
                att_ref[channels(head + own), queried] = (share / norm[:1]).astype(BF16)
            weights = following

    if unfinished:
        fast()
        return
    pl.when(safe)(fast)

    @pl.when(jnp.logical_not(safe))
    def _():
        tiles = length // 256

        def step(t, carry):
            head = t % HEADS
            index = t // HEADS
            cols = pl.ds(pl.multiple_of(index * 256, 256), 256)
            rows = pl.ds(pl.multiple_of(head * WIDTH, WIDTH), WIDTH)
            owner = lax.broadcasted_iota(jnp.int32, (C, 256), 0) // WIDTH
            queries = jnp.where(owner == head, qt_ref[:, cols], jnp.zeros((C, 256), BF16))
            scores, owns = [], []
            for k_ref, _ in sources:
                size = k_ref.shape[0] // count
                owns.append(pl.ds(pl.multiple_of(index // tiles * size, size), size))
                scores.append(dot(k_ref[owns[-1], :], queries))
            tops = [jnp.max(score, axis=0, keepdims=True) for score in scores]
            top = functools.reduce(jnp.maximum, tops)
            mixed = 0.0
            for (_, vt_ref), score, own in zip(sources, scores, owns):
                expo = jnp.exp2(score - top).astype(BF16)
                ones = jnp.ones((16, score.shape[0]), BF16)
                mixed = mixed + dot(jnp.concatenate([vt_ref[rows, own], ones], axis=0), expo)
            att_ref[rows, cols] = (mixed[:WIDTH] / mixed[WIDTH : WIDTH + 1]).astype(BF16)
            return carry

        lax.fori_loop(0, count * tiles * HEADS, step, 0)


def row_kernel(
    edges, halo_rows, rows, wconv, bias, gain, wq_t, wk, wv_t, wout, out_ref,
    taps, hidden, normed, k_ref, qt_ref, vt_ref, att_ref, first, both, sent,
):
    index = pl.program_id(0)
    length = hidden.shape[0]
    part = 128
    above = 2 * index if edges else 0
    if edges:
        at_rows = 3 * index, 1 + index
    else:
        at_rows = 1 + index, 2 + index

    def cells(ref, row, start):
        cols = ref.shape[2]
        return ref[start // cols : (start + part) // cols, row].reshape(part, C)

    flat = (length, C)
    taps[0:8, :] = jnp.zeros((8, 3 * C), F32)
    taps[length + 8 : length + 16, :] = jnp.zeros((8, 3 * C), F32)
    weights = jnp.concatenate([wconv[above], wconv[1], wconv[2 - above]], axis=0)
    def convolve(start):
        around = [cells(halo_rows, index, start)] + [cells(rows, row, start) for row in at_rows]
        total = dot(jnp.concatenate(around, axis=1), weights)
        taps[8 + start : 8 + start + part, :] = total

    convolve(0)
    for start in range(0, length, part):
        if start + part < length:
            convolve(start + part)
        at = 8 + start
        pre = (
            taps[at - 1 : at - 1 + part, 0:C]
            + taps[at : at + part, C : 2 * C]
            + taps[at + 1 : at + 1 + part, 2 * C : 3 * C]
            + bias[...]
        )
        h = (cells(rows, at_rows[0], start).astype(F32) + jax.nn.gelu(pre)).astype(BF16)
        hidden[start : start + part, :] = h
        normed[start : start + part, :] = normalize(h.astype(F32), gain[...])
    rounded, q_square, k_square = project(normed[...], wq_t[...], wk[...], wv_t[...])
    k_ref[...], qt_ref[...], vt_ref[...] = rounded
    safe = q_square * k_square <= SAFE_SQUARE
    attend(safe, [(k_ref, vt_ref)], qt_ref, att_ref, 1, 512, 256, 1)
    result = hidden[...].astype(F32) + dot_tn(att_ref[...], wout[...])

    @pl.when(index == 0)
    def _():
        first[...] = result

    @pl.when(index == 1)
    def _():
        pair = [first[...].reshape(length // 8, 8, C), result.reshape(length // 8, 8, C)]
        both[...] = jnp.concatenate(pair, axis=1).astype(BF16)
        copy = pltpu.make_async_copy(both, out_ref, sent)
        copy.start()
        copy.wait()


def whole(shape):
    return pl.BlockSpec(shape, lambda i: (0,) * len(shape))


def row_call(edges, halo, rows, wconv, bias, gain, wq_t, wk, wv_t, wout):
    devices, _, cols, _ = rows.shape
    length = devices * cols
    weights = [wconv, bias, gain, wq_t, wk, wv_t, wout]
    flops = 2 * length * C * (9 * C + 4 * C) * 2 + 2 * 2 * HEADS * length * length * 512
    return pl.pallas_call(
        functools.partial(row_kernel, edges),
        grid=(2,),
        in_specs=[pl.BlockSpec(memory_space=pltpu.VMEM)] * (2 + len(weights)),
        out_specs=pl.BlockSpec(memory_space=pltpu.HBM),
        out_shape=jax.ShapeDtypeStruct((length // 8, 16, C), BF16),
        scratch_shapes=[
            pltpu.VMEM((length + 16, 3 * C), F32),
            pltpu.VMEM((length, C), BF16),
            pltpu.VMEM((length, C), BF16),
            pltpu.VMEM((length, C), BF16),
            pltpu.VMEM((C, length), BF16),
            pltpu.VMEM((C, length), BF16),
            pltpu.VMEM((C, length), BF16),
            pltpu.VMEM((length, C), F32),
            pltpu.VMEM((length // 8, 16, C), BF16),
            pltpu.SemaphoreType.DMA,
        ],
        cost_estimate=pl.CostEstimate(
            flops=flops, bytes_accessed=8 * length * C, transcendentals=2 * HEADS * length**2
        ),
        compiler_params=pltpu.CompilerParams(vmem_limit_bytes=36 * 2**20),
        name="edge_rows" if edges else "middle_rows",
    )(halo, rows, *weights)


def load_cells(block, left, right):
    cells = block[...].astype(F32).reshape(left.shape[0], C)
    left[...] = cells[:, :128]
    right[...] = cells[:, 128:]


def two_columns(index, length):
    return [pl.ds(2 * index + side, length, stride=8) for side in range(2)]


def project_columns(left, right, gain, wq_t, wk, wv_t, x_ref, k_ref, qt_ref, vt_ref, norms):
    index = pl.program_id(0)
    length = x_ref.shape[0] // 2
    columns = jnp.concatenate(
        [
            jnp.concatenate([left[cells, :], right[cells, :]], axis=1)
            for cells in two_columns(index, length)
        ],
        axis=0,
    )
    x_ref[...] = columns.astype(BF16)
    normed = normalize(columns, gain[...])
    rounded, q_square, k_square = project(normed, wq_t[...], wk[...], wv_t[...])
    k_ref[...], qt_ref[...], vt_ref[...] = rounded

    @pl.when(index == 0)
    def _():
        norms[...] = jnp.zeros(norms.shape, F32)

    norms[0] = jnp.maximum(norms[0], q_square)
    norms[1] = jnp.maximum(norms[1], k_square)


def attend_columns(
    norms, sources, qt_ref, x_ref, wout, att_ref, left, right, out_ref, started=None
):
    index = pl.program_id(0)
    length = x_ref.shape[0] // 2
    q_square, k_squares = jnp.max(norms[0][0]), [jnp.max(norm[1]) for norm in norms]
    safe = q_square * functools.reduce(jnp.maximum, k_squares) <= SAFE_SQUARE
    attend(safe, sources, qt_ref, att_ref, 2, 256, 256, 4, started)
    result = x_ref[...].astype(F32) + dot_tn(att_ref[...], wout[...])
    for side, cells in enumerate(two_columns(index, length)):
        left[cells, :] = result[side * length : (side + 1) * length, :128]
        right[cells, :] = result[side * length : (side + 1) * length, 128:]

    @pl.when(index == 3)
    def _():
        blocks, size, _ = out_ref.shape
        for half, ref in enumerate((left, right)):
            values = ref[...].reshape(size // 16, blocks, 16, 128)
            for block in range(blocks):
                part = values[:, block].reshape(size, 128)
                out_ref[block, :, 128 * half : 128 * half + 128] = part.astype(BF16)


def first_kernel(
    block, gain, wq_t, wk, wv_t, x_ref, k_ref, qt_ref, vt_ref, norms, sums, left, right
):
    @pl.when(pl.program_id(0) == 0)
    def _():
        load_cells(block, left, right)

    project_columns(left, right, gain, wq_t, wk, wv_t, x_ref, k_ref, qt_ref, vt_ref, norms)
    attend(None, [(k_ref, vt_ref)], qt_ref, sums, 2, 256, 256, 2, unfinished=True)


def second_kernel(
    block, gain, wq_t, wk, wv_t, wout, xa_ref, ka_ref, qta_ref, vta_ref, norms_a, sums,
    out_ref, x_ref, k_ref, qt_ref, vt_ref, norms, left, right, left_out, right_out, att_ref,
):
    @pl.when(pl.program_id(0) == 0)
    def _():
        load_cells(block, left, right)

    project_columns(left, right, gain, wq_t, wk, wv_t, x_ref, k_ref, qt_ref, vt_ref, norms)
    sources = [(ka_ref, vta_ref), (k_ref, vt_ref)]
    attend_columns(
        [norms_a, norms], sources, qta_ref, xa_ref, wout, att_ref, left_out, right_out, out_ref, sums
    )


def third_kernel(
    wout, ka_ref, vta_ref, norms_a, x_ref, k_ref, qt_ref, vt_ref, norms, out_ref,
    left, right, att_ref,
):
    sources = [(ka_ref, vta_ref), (k_ref, vt_ref)]
    attend_columns([norms, norms_a], sources, qt_ref, x_ref, wout, att_ref, left, right, out_ref)


def col_calls(gain, wq_t, wk, wv_t, wout, blocks):
    def calls(cells):
        pair = cells // 4
        spec_x = pl.BlockSpec((pair, C), lambda i: (i, 0))
        spec_t = pl.BlockSpec((C, pair), lambda i: (0, i))
        spec_n = whole((2, 8, 128))
        spec_s = pl.BlockSpec((HEADS * STARTED, pair), lambda i: (0, i))
        sums_shape = jax.ShapeDtypeStruct((HEADS * STARTED, cells), F32)
        part_specs = [spec_x, spec_x, spec_t, spec_t, spec_n]
        part_shapes = [
            jax.ShapeDtypeStruct((cells, C), BF16),
            jax.ShapeDtypeStruct((cells, C), BF16),
            jax.ShapeDtypeStruct((C, cells), BF16),
            jax.ShapeDtypeStruct((C, cells), BF16),
            jax.ShapeDtypeStruct((2, 8, 128), F32),
        ]
        out = (blocks, cells // blocks, C)
        out_shape = jax.ShapeDtypeStruct(out, BF16)
        halves = [pltpu.VMEM((cells, 128), F32)] * 2
        att = pltpu.VMEM((C, pair), BF16)
        project_flops = 2 * cells * C * 3 * C
        attend_flops = 2 * 2 * HEADS * cells * (cells // 4) * 256 + 2 * cells * C * C

        def call(kernel, name, args, in_specs, out_specs, out_shapes, scratch, flops, exps):
            return pl.pallas_call(
                kernel,
                grid=(4,),
                in_specs=in_specs,
                out_specs=out_specs,
                out_shape=out_shapes,
                scratch_shapes=scratch,
                cost_estimate=pl.CostEstimate(
                    flops=flops, bytes_accessed=8 * cells * C, transcendentals=exps
                ),
                compiler_params=pltpu.CompilerParams(vmem_limit_bytes=VMEM_LIMIT),
                name=name,
            )(*args)

        weights = [gain, wq_t, wk, wv_t]
        weight_specs = [whole(w.shape) for w in weights]
        wout_spec = whole(wout.shape)
        exps = HEADS * cells * cells // 4

        def first(block):
            return call(
                first_kernel, "first_projections", [block] + weights,
                [pl.BlockSpec(memory_space=pltpu.VMEM)] + weight_specs, part_specs + [spec_s],
                part_shapes + [sums_shape], halves, project_flops + attend_flops // 2, exps // 2,
            )

        def second(block, part):
            results = call(
                second_kernel, "first_queries", [block] + weights + [wout] + list(part),
                [pl.BlockSpec(memory_space=pltpu.VMEM)] + weight_specs + [wout_spec] + part_specs + [spec_s],
                [whole(out)] + part_specs, [out_shape] + part_shapes, halves * 2 + [att],
                project_flops + attend_flops // 2, exps // 2,
            )
            return results[0], results[1:]

        def third(part, other):
            return call(
                third_kernel, "second_queries",
                [wout, part[1], part[3], part[4]] + list(other),
                [wout_spec, spec_x, spec_t, spec_n] + part_specs, whole(out), out_shape,
                halves + [att], attend_flops, exps,
            )

        return first, second, third

    return calls


def split_weights(qkv):
    return qkv[:, :C].T, qkv[:, C : 2 * C], qkv[:, 2 * C :].T


def shards(
    radar_input, conv_weight, conv_bias, row_gain, row_qkv, row_out, col_gain, col_qkv, col_out
):
    gy, gx = lax.axis_size("gy"), lax.axis_size("gx")
    height, cols, _ = radar_input.shape
    wconv = conv_weight.transpose(0, 2, 1, 3).reshape(3, C, 3 * C)
    row_weights = (wconv, conv_bias.reshape(1, C), row_gain.reshape(1, C)) + split_weights(row_qkv)
    col_weights = (col_gain.reshape(1, C),) + split_weights(col_qkv)
    rows = radar_input.reshape(gx, height // gx, cols, C)
    rows = lax.all_to_all(rows, "gx", split_axis=0, concat_axis=0, tiled=True)
    count = gy * gx
    up = [(i, i + 1) for i in range(count - 1)]
    down = [(j, i) for i, j in up]
    above = lax.ppermute(rows[:, 3], ("gy", "gx"), up)
    below = lax.ppermute(rows[:, 0], ("gy", "gx"), down)
    middle = row_call(False, rows, rows, *row_weights, row_out)
    halo = jnp.stack([above, below], axis=1)
    edge = row_call(True, halo, rows, *row_weights, row_out)
    middle = lax.all_to_all(middle, ("gx", "gy"), split_axis=0, concat_axis=0, tiled=True)
    first, second, third = col_calls(*col_weights, col_out, gy)(middle.shape[0] * 16)
    part = first(middle)
    edge = lax.all_to_all(edge, ("gx", "gy"), split_axis=0, concat_axis=0, tiled=True)
    middle, other = second(edge, part)
    middle = lax.all_to_all(middle, "gy", split_axis=0, concat_axis=0, tiled=True)
    edge, middle = lax.optimization_barrier((third(part, other), middle))
    edge = lax.all_to_all(edge, "gy", split_axis=0, concat_axis=0, tiled=True)
    middle, edge = (
        rows.reshape(gy, height // 4, 2, cols // gy, C).transpose(1, 2, 0, 3, 4)
        for rows in (middle, edge)
    )
    result = jnp.concatenate([edge[:, :1], middle, edge[:, 1:]], axis=1)
    return result.reshape(height, cols, C)


def solution(mesh):
    in_specs = (P("gy", "gx", None), P(), P(), P(), P(), P(), P(), P(), P())
    out_specs = P("gy", "gx", None)
    return jax.shard_map(shards, mesh=mesh, in_specs=in_specs, out_specs=out_specs, check_vma=False)
```

```python
import functools

import jax
import jax.numpy as jnp
from jax import lax
from jax.experimental import pallas as pl
from jax.experimental.pallas import tpu as pltpu
from jax.sharding import PartitionSpec as P

HEADS = 8
WIDTH = 32
C = 256
SCORE_SCALE = 1.4426950408889634 / 32**0.5
SAFE_SQUARE = 62.0**2
STARTED = WIDTH + 8
VMEM_LIMIT = 56 * 2**20
F32 = jnp.float32
BF16 = jnp.bfloat16


def dot(a, b):
    return jnp.dot(a, b, preferred_element_type=F32)


def dot_nt(a, b):
    return lax.dot_general(a, b, (((1,), (1,)), ((), ())), preferred_element_type=F32)


def dot_tn(a, b):
    return lax.dot_general(a, b, (((0,), (0,)), ((), ())), preferred_element_type=F32)


def normalize(values, gain):
    center = jnp.mean(values, axis=-1, keepdims=True)
    shifted = values - center
    spread = jnp.mean(shifted * shifted, axis=-1, keepdims=True)
    return (shifted * lax.rsqrt(spread + 1e-05) * gain).astype(BF16)


def project(normed, wq_t, wk, wv_t):
    keys = dot(normed, wk)
    queries = dot_nt(wq_t, normed) * SCORE_SCALE
    values = dot_nt(wv_t, normed)
    q_norms = jnp.sum((queries * queries).reshape(HEADS, WIDTH, normed.shape[0]), axis=1)
    head_of = lax.broadcasted_iota(jnp.int32, (C, 128), 0) // WIDTH
    column = lax.broadcasted_iota(jnp.int32, (C, 128), 1)
    pick = jnp.where(head_of == column, 1.0, 0.0).astype(BF16)
    k_norms = dot((keys * keys).astype(BF16), pick)
    rounded = keys.astype(BF16), queries.astype(BF16), values.astype(BF16)
    return rounded, jnp.max(q_norms), jnp.max(k_norms)


def attend(
    safe, sources, qt_ref, att_ref, count, tile, part, joined, started=None, unfinished=False
):
    length = qt_ref.shape[1] // count

    def channels(head, heads=1):
        return slice(head * WIDTH, (head + heads) * WIDTH)

    def with_ones(vt_ref, head, cells, size, heads=1):
        ones = jnp.ones((16, size), BF16)
        return jnp.concatenate([vt_ref[channels(head, heads), cells], ones], axis=0)

    def fast():
        units = [
            (sequence, start, head)
            for sequence in range(count)
            for start in range(0, length, tile)
            for head in range(0, HEADS, joined)
        ]
        pieces = [
            (k_ref, vt_ref, k_ref.shape[0] // count, start)
            for k_ref, vt_ref in (sources if started is None else sources[-1:])
            for start in range(0, k_ref.shape[0] // count, part)
        ]
        zeros = jnp.zeros((WIDTH, tile), BF16)

        def diagonal(unit):
            sequence, start, head = unit
            base = sequence * length + start
            rows = []
            for own in range(joined):
                queries = qt_ref[channels(head + own), base : base + tile]
                row = [queries if own == other else zeros for other in range(joined)]
                rows.append(jnp.concatenate(row, axis=1))
            return jnp.concatenate(rows, axis=0)

        def weigh(unit, queries, piece):
            sequence, _, head = unit
            k_ref, _, size, key = piece
            cells = slice(sequence * size + key, sequence * size + key + part)
            return jnp.exp2(dot(k_ref[cells, channels(head, joined)], queries)).astype(BF16)

        queries = diagonal(units[0])
        weights = [weigh(units[0], queries, piece) for piece in pieces]
        for at, (sequence, start, head) in enumerate(units):
            following, total = [], None
            if at + 1 < len(units):
                queries = diagonal(units[at + 1])
            for piece, weight in zip(pieces, weights):
                if at + 1 < len(units):
                    following.append(weigh(units[at + 1], queries, piece))
                _, vt_ref, size, key = piece
                cells = slice(sequence * size + key, sequence * size + key + part)
                term = dot(with_ones(vt_ref, head, cells, part, joined), weight)
                total = term if total is None else total + term
            base = sequence * length + start
            queried = slice(base, base + tile)
            for own in range(joined):
                cols = slice(own * tile, (own + 1) * tile)
                share = total[channels(own), cols]
                norm = total[joined * WIDTH : joined * WIDTH + 8, cols]
                at_sum = (head + own) * STARTED
                at_norm = at_sum + WIDTH
                if unfinished:
                    att_ref[at_sum:at_norm, queried] = share
                    att_ref[at_norm : at_norm + 8, queried] = norm
                    continue
                if started is not None:
                    share = share + started[at_sum:at_norm, queried]
                    norm = norm + started[at_norm : at_norm + 8, queried]
                att_ref[channels(head + own), queried] = (share * (1.0 / norm[:1])).astype(BF16)
            weights = following

    if unfinished:
        fast()
        return
    pl.when(safe)(fast)

    @pl.when(jnp.logical_not(safe))
    def _():
        tiles = length // 256

        def step(t, carry):
            head = t % HEADS
            index = t // HEADS
            cols = pl.ds(pl.multiple_of(index * 256, 256), 256)
            rows = pl.ds(pl.multiple_of(head * WIDTH, WIDTH), WIDTH)
            owner = lax.broadcasted_iota(jnp.int32, (C, 256), 0) // WIDTH
            queries = jnp.where(owner == head, qt_ref[:, cols], jnp.zeros((C, 256), BF16))
            scores, owns = [], []
            for k_ref, _ in sources:
                size = k_ref.shape[0] // count
                owns.append(pl.ds(pl.multiple_of(index // tiles * size, size), size))
                scores.append(dot(k_ref[owns[-1], :], queries))
            tops = [jnp.max(score, axis=0, keepdims=True) for score in scores]
            top = functools.reduce(jnp.maximum, tops)
            mixed = 0.0
            for (_, vt_ref), score, own in zip(sources, scores, owns):
                expo = jnp.exp2(score - top).astype(BF16)
                ones = jnp.ones((16, score.shape[0]), BF16)
                mixed = mixed + dot(jnp.concatenate([vt_ref[rows, own], ones], axis=0), expo)
            att_ref[rows, cols] = (mixed[:WIDTH] / mixed[WIDTH : WIDTH + 1]).astype(BF16)
            return carry

        lax.fori_loop(0, count * tiles * HEADS, step, 0)


def row_kernel(
    edges, halo_rows, rows, wconv, bias, gain, wq_t, wk, wv_t, wout, out_ref,
    taps, hidden, normed, k_ref, qt_ref, vt_ref, att_ref, first, both, sent,
):
    index = pl.program_id(0)
    length = hidden.shape[0]
    part = 128
    above = 2 * index if edges else 0
    if edges:
        at_rows = 3 * index, 1 + index
    else:
        at_rows = 1 + index, 2 + index

    def cells(ref, row, start):
        cols = ref.shape[2]
        return ref[start // cols : (start + part) // cols, row].reshape(part, C)

    flat = (length, C)
    taps[0:8, :] = jnp.zeros((8, 3 * C), F32)
    taps[length + 8 : length + 16, :] = jnp.zeros((8, 3 * C), F32)
    weights = jnp.concatenate([wconv[above], wconv[1], wconv[2 - above]], axis=0)
    def convolve(start):
        around = [cells(halo_rows, index, start)] + [cells(rows, row, start) for row in at_rows]
        total = dot(jnp.concatenate(around, axis=1), weights)
        taps[8 + start : 8 + start + part, :] = total

    convolve(0)
    for start in range(0, length, part):
        if start + part < length:
            convolve(start + part)
        at = 8 + start
        pre = (
            taps[at - 1 : at - 1 + part, 0:C]
            + taps[at : at + part, C : 2 * C]
            + taps[at + 1 : at + 1 + part, 2 * C : 3 * C]
            + bias[...]
        )
        h = (cells(rows, at_rows[0], start).astype(F32) + jax.nn.gelu(pre)).astype(BF16)
        hidden[start : start + part, :] = h
        normed[start : start + part, :] = normalize(h.astype(F32), gain[...])
    rounded, q_square, k_square = project(normed[...], wq_t[...], wk[...], wv_t[...])
    k_ref[...], qt_ref[...], vt_ref[...] = rounded
    safe = q_square * k_square <= SAFE_SQUARE
    attend(safe, [(k_ref, vt_ref)], qt_ref, att_ref, 1, 512, 256, 1)
    result = hidden[...].astype(F32) + dot_tn(att_ref[...], wout[...])

    @pl.when(index == 0)
    def _():
        first[...] = result

    @pl.when(index == 1)
    def _():
        pair = [first[...].reshape(length // 8, 8, C), result.reshape(length // 8, 8, C)]
        both[...] = jnp.concatenate(pair, axis=1).astype(BF16)
        copy = pltpu.make_async_copy(both, out_ref, sent)
        copy.start()
        copy.wait()


def whole(shape):
    return pl.BlockSpec(shape, lambda i: (0,) * len(shape))


def row_call(edges, halo, rows, wconv, bias, gain, wq_t, wk, wv_t, wout):
    devices, _, cols, _ = rows.shape
    length = devices * cols
    weights = [wconv, bias, gain, wq_t, wk, wv_t, wout]
    flops = 2 * length * C * (9 * C + 4 * C) * 2 + 2 * 2 * HEADS * length * length * 512
    return pl.pallas_call(
        functools.partial(row_kernel, edges),
        grid=(2,),
        in_specs=[pl.BlockSpec(memory_space=pltpu.VMEM)] * (2 + len(weights)),
        out_specs=pl.BlockSpec(memory_space=pltpu.HBM),
        out_shape=jax.ShapeDtypeStruct((length // 8, 16, C), BF16),
        scratch_shapes=[
            pltpu.VMEM((length + 16, 3 * C), F32),
            pltpu.VMEM((length, C), BF16),
            pltpu.VMEM((length, C), BF16),
            pltpu.VMEM((length, C), BF16),
            pltpu.VMEM((C, length), BF16),
            pltpu.VMEM((C, length), BF16),
            pltpu.VMEM((C, length), BF16),
            pltpu.VMEM((length, C), F32),
            pltpu.VMEM((length // 8, 16, C), BF16),
            pltpu.SemaphoreType.DMA,
        ],
        cost_estimate=pl.CostEstimate(
            flops=flops, bytes_accessed=8 * length * C, transcendentals=2 * HEADS * length**2
        ),
        compiler_params=pltpu.CompilerParams(vmem_limit_bytes=36 * 2**20),
        name="edge_rows" if edges else "middle_rows",
    )(halo, rows, *weights)


def load_cells(block, left, right):
    cells = block[...].astype(F32).reshape(left.shape[0], C)
    left[...] = cells[:, :128]
    right[...] = cells[:, 128:]


def two_columns(index, length):
    return [pl.ds(2 * index + side, length, stride=8) for side in range(2)]


def project_columns(left, right, gain, wq_t, wk, wv_t, x_ref, k_ref, qt_ref, vt_ref, norms):
    index = pl.program_id(0)
    length = x_ref.shape[0] // 2
    columns = jnp.concatenate(
        [
            jnp.concatenate([left[cells, :], right[cells, :]], axis=1)
            for cells in two_columns(index, length)
        ],
        axis=0,
    )
    x_ref[...] = columns.astype(BF16)
    normed = normalize(columns, gain[...])
    rounded, q_square, k_square = project(normed, wq_t[...], wk[...], wv_t[...])
    k_ref[...], qt_ref[...], vt_ref[...] = rounded

    @pl.when(index == 0)
    def _():
        norms[...] = jnp.zeros(norms.shape, F32)

    norms[0] = jnp.maximum(norms[0], q_square)
    norms[1] = jnp.maximum(norms[1], k_square)


def attend_columns(
    norms, sources, qt_ref, x_ref, wout, att_ref, left, right, out_ref, started=None
):
    index = pl.program_id(0)
    length = x_ref.shape[0] // 2
    q_square, k_squares = jnp.max(norms[0][0]), [jnp.max(norm[1]) for norm in norms]
    safe = q_square * functools.reduce(jnp.maximum, k_squares) <= SAFE_SQUARE
    attend(safe, sources, qt_ref, att_ref, 2, 256, 256, 4, started)
    result = x_ref[...].astype(F32) + dot_tn(att_ref[...], wout[...])
    for side, cells in enumerate(two_columns(index, length)):
        left[cells, :] = result[side * length : (side + 1) * length, :128]
        right[cells, :] = result[side * length : (side + 1) * length, 128:]

    @pl.when(index == 3)
    def _():
        blocks, size, _ = out_ref.shape
        for half, ref in enumerate((left, right)):
            values = ref[...].reshape(size // 16, blocks, 16, 128)
            for block in range(blocks):
                part = values[:, block].reshape(size, 128)
                out_ref[block, :, 128 * half : 128 * half + 128] = part.astype(BF16)


def first_kernel(
    block, gain, wq_t, wk, wv_t, x_ref, k_ref, qt_ref, vt_ref, norms, sums, left, right
):
    @pl.when(pl.program_id(0) == 0)
    def _():
        load_cells(block, left, right)

    project_columns(left, right, gain, wq_t, wk, wv_t, x_ref, k_ref, qt_ref, vt_ref, norms)
    attend(None, [(k_ref, vt_ref)], qt_ref, sums, 2, 256, 256, 2, unfinished=True)


def second_kernel(
    block, gain, wq_t, wk, wv_t, wout, xa_ref, ka_ref, qta_ref, vta_ref, norms_a, sums,
    out_ref, x_ref, k_ref, qt_ref, vt_ref, norms, left, right, left_out, right_out, att_ref,
):
    @pl.when(pl.program_id(0) == 0)
    def _():
        load_cells(block, left, right)

    project_columns(left, right, gain, wq_t, wk, wv_t, x_ref, k_ref, qt_ref, vt_ref, norms)
    sources = [(ka_ref, vta_ref), (k_ref, vt_ref)]
    attend_columns(
        [norms_a, norms], sources, qta_ref, xa_ref, wout, att_ref, left_out, right_out, out_ref, sums
    )


def third_kernel(
    wout, ka_ref, vta_ref, norms_a, x_ref, k_ref, qt_ref, vt_ref, norms, out_ref,
    left, right, att_ref,
):
    sources = [(ka_ref, vta_ref), (k_ref, vt_ref)]
    attend_columns([norms, norms_a], sources, qt_ref, x_ref, wout, att_ref, left, right, out_ref)


def col_calls(gain, wq_t, wk, wv_t, wout, blocks):
    def calls(cells):
        pair = cells // 4
        spec_x = pl.BlockSpec((pair, C), lambda i: (i, 0))
        spec_t = pl.BlockSpec((C, pair), lambda i: (0, i))
        spec_n = whole((2, 8, 128))
        spec_s = pl.BlockSpec((HEADS * STARTED, pair), lambda i: (0, i))
        sums_shape = jax.ShapeDtypeStruct((HEADS * STARTED, cells), F32)
        part_specs = [spec_x, spec_x, spec_t, spec_t, spec_n]
        part_shapes = [
            jax.ShapeDtypeStruct((cells, C), BF16),
            jax.ShapeDtypeStruct((cells, C), BF16),
            jax.ShapeDtypeStruct((C, cells), BF16),
            jax.ShapeDtypeStruct((C, cells), BF16),
            jax.ShapeDtypeStruct((2, 8, 128), F32),
        ]
        out = (blocks, cells // blocks, C)
        out_shape = jax.ShapeDtypeStruct(out, BF16)
        halves = [pltpu.VMEM((cells, 128), F32)] * 2
        att = pltpu.VMEM((C, pair), BF16)
        project_flops = 2 * cells * C * 3 * C
        attend_flops = 2 * 2 * HEADS * cells * (cells // 4) * 256 + 2 * cells * C * C

        def call(kernel, name, args, in_specs, out_specs, out_shapes, scratch, flops, exps):
            return pl.pallas_call(
                kernel,
                grid=(4,),
                in_specs=in_specs,
                out_specs=out_specs,
                out_shape=out_shapes,
                scratch_shapes=scratch,
                cost_estimate=pl.CostEstimate(
                    flops=flops, bytes_accessed=8 * cells * C, transcendentals=exps
                ),
                compiler_params=pltpu.CompilerParams(vmem_limit_bytes=VMEM_LIMIT),
                name=name,
            )(*args)

        weights = [gain, wq_t, wk, wv_t]
        weight_specs = [whole(w.shape) for w in weights]
        wout_spec = whole(wout.shape)
        exps = HEADS * cells * cells // 4

        def first(block):
            return call(
                first_kernel, "first_projections", [block] + weights,
                [pl.BlockSpec(memory_space=pltpu.VMEM)] + weight_specs, part_specs + [spec_s],
                part_shapes + [sums_shape], halves, project_flops + attend_flops // 2, exps // 2,
            )

        def second(block, part):
            results = call(
                second_kernel, "first_queries", [block] + weights + [wout] + list(part),
                [pl.BlockSpec(memory_space=pltpu.VMEM)] + weight_specs + [wout_spec] + part_specs + [spec_s],
                [whole(out)] + part_specs, [out_shape] + part_shapes, halves * 2 + [att],
                project_flops + attend_flops // 2, exps // 2,
            )
            return results[0], results[1:]

        def third(part, other):
            return call(
                third_kernel, "second_queries",
                [wout, part[1], part[3], part[4]] + list(other),
                [wout_spec, spec_x, spec_t, spec_n] + part_specs, whole(out), out_shape,
                halves + [att], attend_flops, exps,
            )

        return first, second, third

    return calls


def split_weights(qkv):
    return qkv[:, :C].T, qkv[:, C : 2 * C], qkv[:, 2 * C :].T


def shards(
    radar_input, conv_weight, conv_bias, row_gain, row_qkv, row_out, col_gain, col_qkv, col_out
):
    gy, gx = lax.axis_size("gy"), lax.axis_size("gx")
    height, cols, _ = radar_input.shape
    wconv = conv_weight.transpose(0, 2, 1, 3).reshape(3, C, 3 * C)
    row_weights = (wconv, conv_bias.reshape(1, C), row_gain.reshape(1, C)) + split_weights(row_qkv)
    col_weights = (col_gain.reshape(1, C),) + split_weights(col_qkv)
    rows = radar_input.reshape(gx, height // gx, cols, C)
    rows = lax.all_to_all(rows, "gx", split_axis=0, concat_axis=0, tiled=True)
    count = gy * gx
    up = [(i, i + 1) for i in range(count - 1)]
    down = [(j, i) for i, j in up]
    above = lax.ppermute(rows[:, 3], ("gy", "gx"), up)
    below = lax.ppermute(rows[:, 0], ("gy", "gx"), down)
    middle = row_call(False, rows, rows, *row_weights, row_out)
    halo = jnp.stack([above, below], axis=1)
    edge = row_call(True, halo, rows, *row_weights, row_out)
    middle = lax.all_to_all(middle, ("gx", "gy"), split_axis=0, concat_axis=0, tiled=True)
    first, second, third = col_calls(*col_weights, col_out, gy)(middle.shape[0] * 16)
    part = first(middle)
    edge = lax.all_to_all(edge, ("gx", "gy"), split_axis=0, concat_axis=0, tiled=True)
    middle, other = second(edge, part)
    middle = lax.all_to_all(middle, "gy", split_axis=0, concat_axis=0, tiled=True)
    edge, middle = lax.optimization_barrier((third(part, other), middle))
    edge = lax.all_to_all(edge, "gy", split_axis=0, concat_axis=0, tiled=True)
    middle, edge = (
        rows.reshape(gy, height // 4, 2, cols // gy, C).transpose(1, 2, 0, 3, 4)
        for rows in (middle, edge)
    )
    result = jnp.concatenate([edge[:, :1], middle, edge[:, 1:]], axis=1)
    return result.reshape(height, cols, C)


def solution(mesh):
    in_specs = (P("gy", "gx", None), P(), P(), P(), P(), P(), P(), P(), P())
    out_specs = P("gy", "gx", None)
    return jax.shard_map(shards, mesh=mesh, in_specs=in_specs, out_specs=out_specs, check_vma=False)
```
